256 devices in a mesh: gx: 32 (over x_hi, z, core), gy: 8 (over y, x_lo).
Axes of the slice: x: 4 (x_hi: 2, x_lo: 2; x = x_hi * 2 + x_lo), y: 4, z: 8, core: 2. Of those that a mesh axis runs over, the one named last changes fastest.
Arguments:
- fields: float32 [64, 2304, 2000], P(None, 'gx', 'gy'), may hold values from -6 to 6
Outputs:
- spectrum: float32 [2, 64, 1152, 2000], P(None, 'gx', 'gy')
The draws below stay inside these ranges and needn't reach their ends.
All inputs are finite; a program needn't handle non-finite values.
Results may differ from the reference program's by a relative error of at most 0.00007.
Values sent between devices are 32-bit elements; how exact they have to be, the bound alone decides.
No kernel may reach another device: no remote copies, remote signals or barrier semaphores. Data moves between devices by JAX's collectives and lax.ppermute only.
A program may use at most 128 MiB of HBM per device.

```python
import math
import jax
import jax.numpy as jnp

NX = 2304
NY = 2000
KX = 1152
FIELDS = 64


def shard_levels(key, shape, cuts, low, largest):
    def one(axis_at, parts):
        steps = jax.random.uniform(jax.random.fold_in(jax.random.fold_in(key, 6), axis_at), (parts,), jnp.float32, low / len(cuts), largest / len(cuts))
        return jnp.repeat(jnp.exp(steps), shape[axis_at] // parts).reshape((-1,) + (1,) * (len(shape) - axis_at - 1))

    gain = one(*cuts[0])
    for cut in cuts[1:]:
        gain = gain * one(*cut)
    return gain


def scatter_about(key, shape, scale, most, split=(), dtype=jnp.bfloat16):
    array = jax.random.normal(key, shape, jnp.float32) * scale
    if len(split) > 0:
        array = shard_levels(key, shape, split, -0.22, 0.18) * array
    return jnp.clip(array, min=-most, max=most).astype(dtype)


def setup_inputs(seed: int = 0) -> dict:
    streams_of = jax.random.split(jax.random.key(seed), 2)
    fields = scatter_about(streams_of[0], (FIELDS, NX, NY), 1.0, 6.0, ((1, 32), (2, 8)), jnp.float32)
    return dict(fields=fields)


def reference(fields):
    spectra = jnp.fft.rfft(fields, axis=1)[:, :KX, :] / math.sqrt(NX)
    spectra = jnp.fft.fft(spectra, axis=2) / math.sqrt(NY)
    return jnp.stack([jnp.real(spectra), jnp.imag(spectra)]).astype(jnp.float32)
```

```python
import functools
import math

import jax
import jax.numpy as jnp
import ml_dtypes
import numpy as np
from jax import lax
from jax.experimental import pallas as pl
from jax.experimental.pallas import tpu as pltpu
from jax.sharding import PartitionSpec as P

NX = 2304
NY = 2000
KX = 1152
HALF = NX // 2
STRIP = 72
LANES = 128
ROWS = 250
NJ = 8
NZ = 8
VMEM = 48 * 1024 * 1024


def split_table(table):
    high = table.astype(np.float32).astype(ml_dtypes.bfloat16)
    low = (table - high.astype(np.float64)).astype(np.float32).astype(ml_dtypes.bfloat16)
    return high, low


@functools.cache
def x_table():
    b = np.arange(HALF)
    steps = []
    for p in range(2):
        for m in range(2):
            block = np.arange(4)[:, None] + 4 * m
            k = (144 * block + 2 * np.arange(STRIP)[None, :] + p).reshape(-1)
            angle = 2.0 * np.pi / NX * ((k[:, None] * b[None, :]) % NX)
            both = np.stack([np.cos(angle).reshape(4, STRIP, HALF), -np.sin(angle).reshape(4, STRIP, HALF)], axis=1)
            high, low = split_table(both.reshape(-1, HALF) / math.sqrt(NX))
            steps.append(np.concatenate([high, low], axis=0))
    return np.stack(steps)


@functools.cache
def y_tables():
    b = np.arange(2 * LANES)
    twist = 2.0 * np.pi / NY * ((np.arange(NJ)[:, None] * b[None, :]) % NY)
    twiddle = np.stack([np.cos(twist), np.sin(twist)], axis=1)
    twiddle = twiddle.reshape(NJ, 2, 2, LANES).transpose(2, 0, 1, 3).astype(np.float32)
    d = np.arange(2 * LANES)
    angle = 2.0 * np.pi / ROWS * ((b[:, None] * d[None, :]) % ROWS)
    keep = ((b < ROWS)[:, None] & (d < ROWS)[None, :]).astype(np.float64) / math.sqrt(NY)
    cosine, sine = np.cos(angle) * keep, np.sin(angle) * keep
    from_real = np.concatenate([cosine, -sine], axis=1)
    from_imag = np.concatenate([sine, cosine], axis=1)
    rows = np.concatenate([from_real[:LANES], from_imag[:LANES], from_real[LANES:], from_imag[LANES:]], axis=0)
    main = np.stack(split_table(rows))
    weave = np.zeros((4, 2 * LANES, 2 * LANES), np.float32)
    for t in range(4):
        for upper in range(2):
            for lane in range(LANES):
                c = 4 * upper + (lane // 32 - t) % 4
                weave[t, upper * LANES + lane, 8 * (lane % 32) + c] = 1.0
    return twiddle, main, weave.astype(ml_dtypes.bfloat16)


def compiler_params():
    return pltpu.CompilerParams(vmem_limit_bytes=VMEM)


def store_lanes(out, value, half):
    if half == 0:
        out[...] = value
    else:
        out[...] = jnp.zeros(out.shape, out.dtype)
        out[..., : ROWS - LANES] = value


def pack_first(fields):
    def kernel(a, out):
        for hi in range(2):
            for core in range(2):
                out[hi, :, core] = a[hi, :, 2 * core]

    return pl.pallas_call(
        kernel,
        grid=(4,),
        out_shape=jax.ShapeDtypeStruct((2, NZ, 2, STRIP, LANES), jnp.float32),
        in_specs=[pl.BlockSpec((2, 2, 4, STRIP, LANES), lambda i: (0, i, 0, 0, 0))],
        out_specs=pl.BlockSpec((2, 2, 2, STRIP, LANES), lambda i: (0, i, 0, 0, 0)),
        compiler_params=compiler_params(),
        name="pack_first",
    )(fields)


CHUNKS = ((0, 1), (1, 0), (1, 1))
PARTNERS = ((0, 0), (0, 1), (1, 0), (1, 1))


def pack_rest(place, fields):
    def kernel(place, a, *outs):
        hi, core = place[0], place[2]
        index = 0
        for field, half in CHUNKS:
            for dh, dc in PARTNERS:
                to_hi = lax.rem(hi + dh, 2)
                to_core = lax.rem(core + dc, 2)
                lanes = slice(0, LANES) if half == 0 else slice(LANES, ROWS)
                store_lanes(outs[index], a[pl.ds(to_hi, 1), 0, pl.ds(2 * to_core + field, 1), :, lanes][0], half)
                index += 1

    shape = jax.ShapeDtypeStruct((NZ, STRIP, LANES), jnp.float32)
    spec = pl.BlockSpec((1, STRIP, LANES), lambda i, place: (i, 0, 0))
    return pl.pallas_call(
        kernel,
        grid_spec=pltpu.PrefetchScalarGridSpec(
            num_scalar_prefetch=1,
            grid=(NZ,),
            in_specs=[pl.BlockSpec((2, 1, 4, STRIP, ROWS), lambda i, place: (0, i, 0, 0, 0))],
            out_specs=[spec] * 12,
        ),
        out_shape=[shape] * 12,
        compiler_params=compiler_params(),
        name="pack_rest",
    )(place, fields)


def pack_z(place, parts):
    def kernel(place, *refs):
        sources, outs, sem = refs[:4], refs[4:11], refs[11]
        copies = []
        for dz in range(1, NZ):
            to_z = lax.rem(place[1] + dz, NZ)
            for i in range(4):
                copies.append(pltpu.make_async_copy(sources[i].at[to_z], outs[dz - 1].at[i], sem))
        for copy in copies:
            copy.start()
        for copy in copies:
            copy.wait()

    shape = jax.ShapeDtypeStruct((4, STRIP, LANES), jnp.float32)
    anywhere = pl.BlockSpec(memory_space=pl.ANY)
    return pl.pallas_call(
        kernel,
        in_specs=[pl.BlockSpec(memory_space=pltpu.SMEM)] + [anywhere] * 4,
        out_specs=[anywhere] * 7,
        out_shape=[shape] * 7,
        scratch_shapes=[pltpu.SemaphoreType.DMA],
        compiler_params=compiler_params(),
        name="pack_z",
    )(place, *parts)


def x_transform(place, pieces):
    whole = len(pieces) == 1

    def kernel(place, *refs):
        sources = refs[: len(pieces)]
        table, out, columns, folded, sem = refs[len(pieces) :]
        step = pl.program_id(0)

        @pl.when(step == 0)
        def _():
            copies = []
            if whole:
                copies.append(pltpu.make_async_copy(sources[0], columns, sem))
            else:
                hi, z, core = place[0], place[1], place[2]
                for i, (dh, dc) in enumerate(PARTNERS):
                    from_hi = lax.rem(hi + dh, 2)
                    from_core = lax.rem(core + dc, 2)
                    for dz in range(NZ):
                        from_z = lax.rem(z + NZ - dz, NZ)
                        source = sources[i].at[z] if dz == 0 else sources[3 + dz].at[i]
                        start = pl.multiple_of(STRIP * (from_hi * 16 + from_z * 2 + from_core), 8)
                        copies.append(pltpu.make_async_copy(source, columns.at[pl.ds(start, STRIP)], sem))
            for copy in copies:
                copy.start()
            for copy in copies:
                copy.wait()
            first = columns[:HALF]
            second = columns[HALF:]
            for p, value in enumerate((first + second, first - second)):
                high = value.astype(jnp.bfloat16)
                low = (value - high.astype(jnp.float32)).astype(jnp.bfloat16)
                folded[p, :, :LANES] = high
                folded[p, :, LANES:] = low

        product = jnp.dot(table[0], folded[step // 2], preferred_element_type=jnp.float32)
        upper = product[: HALF // 2]
        lower = product[HALF // 2 :]
        total = upper[:, :LANES] + (upper[:, LANES:] + lower[:, :LANES])
        out[...] = total.reshape(4, 2, 1, STRIP, LANES)

    anywhere = pl.BlockSpec(memory_space=pl.ANY)
    return pl.pallas_call(
        kernel,
        grid_spec=pltpu.PrefetchScalarGridSpec(
            num_scalar_prefetch=1,
            grid=(4,),
            in_specs=[anywhere] * len(pieces) + [pl.BlockSpec((1, HALF, HALF), lambda s, place: (s, 0, 0))],
            out_specs=pl.BlockSpec((4, 2, 1, STRIP, LANES), lambda s, place: (s % 2, 0, s // 2, 0, 0)),
            scratch_shapes=[
                pltpu.VMEM((NX, LANES), jnp.float32),
                pltpu.VMEM((2, HALF, 2 * LANES), jnp.bfloat16),
                pltpu.SemaphoreType.DMA,
            ],
        ),
        out_shape=jax.ShapeDtypeStruct((NJ, 2, 2, STRIP, LANES), jnp.float32),
        compiler_params=compiler_params(),
        name="x_transform",
    )(place, *pieces, jnp.asarray(x_table()))


def eight_point(re, im):
    def add(a, b):
        return a[0] + b[0], a[1] + b[1]

    def sub(a, b):
        return a[0] - b[0], a[1] - b[1]

    def four(v):
        s, d = add(v[0], v[2]), sub(v[0], v[2])
        t, e = add(v[1], v[3]), sub(v[1], v[3])
        turned = e[1], -e[0]
        return add(s, t), add(d, turned), sub(s, t), sub(d, turned)

    values = list(zip(re, im))
    even = four(values[0::2])
    odd = four(values[1::2])
    root = math.sqrt(0.5)
    o1 = (odd[1][0] + odd[1][1]) * root, (odd[1][1] - odd[1][0]) * root
    o2 = odd[2][1], -odd[2][0]
    o3 = (odd[3][1] - odd[3][0]) * root, (odd[3][0] + odd[3][1]) * -root
    odd = odd[0], o1, o2, o3
    return [add(e, o) for e, o in zip(even, odd)] + [sub(e, o) for e, o in zip(even, odd)]


TILE = 16


def y_kernel(first, second, twiddle, main, weave, *refs):
    out, high, low, mixed, woven = refs[-5:]
    for half, source in enumerate((first, second)):

        def fold(i, carry, half=half, source=source):
            rows = pl.ds(pl.multiple_of(i * TILE, TILE), TILE)
            re = [source[j, 0, rows, :] for j in range(NJ)]
            im = [source[j, 1, rows, :] for j in range(NJ)]
            for c, (a, b) in enumerate(eight_point(re, im)):
                if c > 0:
                    cosine = twiddle[half, c, 0:1, :]
                    sine = twiddle[half, c, 1:2, :]
                    a, b = a * cosine + b * sine, b * cosine - a * sine
                for comp, value in enumerate((a, b)):
                    lanes = slice((2 * half + comp) * LANES, (2 * half + comp + 1) * LANES)
                    top = value.astype(jnp.bfloat16)
                    high[c, rows, lanes] = top
                    low[c, rows, lanes] = (value - top.astype(jnp.float32)).astype(jnp.bfloat16)
            return carry

        lax.fori_loop(0, 144 // TILE, fold, 0)

    for c in range(NJ):
        a = high[c]
        value = (
            jnp.dot(a, main[0], preferred_element_type=jnp.float32)
            + jnp.dot(low[c], main[0], preferred_element_type=jnp.float32)
            + jnp.dot(a, main[1], preferred_element_type=jnp.float32)
        )
        for part in range(4):
            piece = value[:, part * LANES : (part + 1) * LANES]
            if c % 4 > 0:
                piece = pltpu.roll(piece, 32 * (c % 4), 1)
            for p in range(2):
                mixed[c, part, pl.ds(p, STRIP, stride=2), :] = piece[p * STRIP : (p + 1) * STRIP]

    slot = lax.broadcasted_iota(jnp.int32, (144, LANES), 1) // 32
    for t in range(4):
        for comp in range(2):
            for upper in range(2):
                part = 2 * comp + upper
                for group in range(2):
                    value = mixed[4 * group, part]
                    for c in range(1, 4):
                        value = jnp.where(slot == (c + t) % 4, mixed[4 * group + c, part], value)
                    top = value.astype(jnp.bfloat16)
                    start = part * 144
                    columns = slice(group * LANES, (group + 1) * LANES)
                    woven[start : start + 144, columns] = top
                    woven[start + 576 : start + 720, columns] = (value - top.astype(jnp.float32)).astype(jnp.bfloat16)
        product = jnp.dot(woven[...], weave[t], preferred_element_type=jnp.float32)
        product = product[:576] + product[576:]
        for comp in range(2):
            for upper in range(2):
                tile = 4 * upper + t
                width = min(256, NY - 256 * tile)
                start = (2 * comp + upper) * 144
                out[comp, 0, :, 256 * tile : 256 * tile + width] = product[start : start + 144, :width]


def y_transform(field, halves, before):
    twiddle, main, weave = y_tables()
    whole = pl.BlockSpec(memory_space=pltpu.VMEM)
    inputs = [*halves, jnp.asarray(twiddle), jnp.asarray(main), jnp.asarray(weave)]
    block = pl.BlockSpec((2, 1, 144, NY), lambda i: (0, field, 0, 0))

    def full(array):
        zeros = (0,) * array.ndim
        return pl.BlockSpec(array.shape, lambda i: zeros)

    in_specs = [full(array) for array in inputs]
    aliases = {}
    if before is not None:
        aliases = {len(inputs): 0}
        inputs.append(before)
        in_specs.append(pl.BlockSpec(memory_space=pl.ANY))
    return pl.pallas_call(
        y_kernel,
        grid=(1,),
        in_specs=in_specs,
        out_specs=block,
        out_shape=jax.ShapeDtypeStruct((2, 2, 144, NY), jnp.float32),
        scratch_shapes=[
            pltpu.VMEM((NJ, 144, 512), jnp.bfloat16),
            pltpu.VMEM((NJ, 144, 512), jnp.bfloat16),
            pltpu.VMEM((NJ, 4, 144, LANES), jnp.float32),
            pltpu.VMEM((1152, 256), jnp.bfloat16),
        ],
        input_output_aliases=aliases,
        compiler_params=compiler_params(),
        name="y_transform",
    )(*inputs)


def shift(dh, dz, dc):
    pairs = []
    for hi in range(2):
        for z in range(NZ):
            for core in range(2):
                to = (hi + dh) % 2 * 16 + (z + dz) % NZ * 2 + (core + dc) % 2
                pairs.append((hi * 16 + z * 2 + core, to))
    return pairs


def over_y(blocks):
    blocks = blocks.reshape(NJ, 2, 144, LANES)
    return lax.all_to_all(blocks, "gy", split_axis=0, concat_axis=0, tiled=True)


Z_ORDER = (4, 3, 5, 2, 6, 1, 7)


def body(fields):
    me = lax.axis_index("gx")
    place = jnp.stack([me // 16, me // 2 % NZ, me % 2]).astype(jnp.int32)
    fields = fields.reshape(2, NZ, 4, STRIP, ROWS)
    first = pack_first(fields).reshape(32, STRIP, LANES)
    first = lax.all_to_all(first, "gx", split_axis=0, concat_axis=0, tiled=True)
    packed = pack_rest(place, fields)
    spectra = [over_y(x_transform(place, [first.reshape(NX, LANES)]))]
    for chunk in range(3):
        own, *away = packed[4 * chunk : 4 * chunk + 4]
        parts = [own]
        for (dh, dc), part in zip(PARTNERS[1:], away):
            parts.append(lax.ppermute(part, "gx", shift(dh, 0, dc)))
        sends = pack_z(place, parts)
        received = [None] * 7
        for dz in Z_ORDER:
            received[dz - 1] = lax.ppermute(sends[dz - 1], "gx", shift(0, dz, 0))
        spectra.append(over_y(x_transform(place, parts + received)))
    result = y_transform(0, spectra[:2], None)
    return y_transform(1, spectra[2:], result)


def solution(mesh):
    in_specs = (P(None, "gx", "gy"),)
    out_specs = P(None, "gx", "gy", None)
    return jax.shard_map(body, mesh=mesh, in_specs=in_specs, out_specs=out_specs, check_vma=False)
```

```python
import functools
import math

import jax
import jax.numpy as jnp
import ml_dtypes
import numpy as np
from jax import lax
from jax.experimental import pallas as pl
from jax.experimental.pallas import tpu as pltpu
from jax.sharding import PartitionSpec as P

NX = 2304
NY = 2000
KX = 1152
NQ = 9
STRIP = 72
LANES = 128
ROWS = 250
NJ = 8
NZ = 8
TILE = 16
VMEM = 63 * 1000 * 1000


def split_table(table):
    high = table.astype(np.float32).astype(ml_dtypes.bfloat16)
    low = (table - high.astype(np.float64)).astype(np.float32).astype(ml_dtypes.bfloat16)
    return high, low


@functools.cache
def x_table():
    b = np.arange(LANES)
    steps = []
    for q in range(NQ):
        groups = np.array([0, 9] if q == 0 else [q, 18 - q])
        k = 144 * np.arange(NJ)[:, None, None] + groups[None, :, None] + 18 * np.arange(8)[None, None, :]
        angle = 2.0 * np.pi / NX * ((k[..., None] * b) % NX)
        cosine, sine = np.cos(angle), np.sin(angle)
        rows = np.zeros((NJ, 2, 2, 8, 2, LANES))
        for group in range(2):
            if q == 0:
                rows[:, group, 0, :, group] = cosine[:, group]
                rows[:, group, 1, :, group] = -sine[:, group]
            else:
                sign = 1 - 2 * group
                rows[:, group, 0, :, 0] = cosine[:, group]
                rows[:, group, 0, :, 1] = sign * sine[:, group]
                rows[:, group, 1, :, 0] = -sine[:, group]
                rows[:, group, 1, :, 1] = sign * cosine[:, group]
        steps.append(np.concatenate(split_table(rows.reshape(256, 256) / math.sqrt(NX))))
    return np.stack(steps)


@functools.cache
def y_tables():
    b = np.arange(2 * LANES)
    twist = 2.0 * np.pi / NY * ((np.arange(NJ)[:, None] * b[None, :]) % NY)
    twiddle = np.stack([np.cos(twist), np.sin(twist)], axis=1)
    twiddle = twiddle.reshape(NJ, 2, 2, LANES).transpose(2, 0, 1, 3).astype(np.float32)
    d = np.arange(2 * LANES)
    angle = 2.0 * np.pi / ROWS * ((b[:, None] * d[None, :]) % ROWS)
    keep = ((b < ROWS)[:, None] & (d < ROWS)[None, :]).astype(np.float64) / math.sqrt(NY)
    cosine, sine = np.cos(angle) * keep, np.sin(angle) * keep
    from_real = np.concatenate([cosine, -sine], axis=1)
    from_imag = np.concatenate([sine, cosine], axis=1)
    rows = np.concatenate([from_real[:LANES], from_imag[:LANES], from_real[LANES:], from_imag[LANES:]], axis=0)
    main = np.stack(split_table(rows))
    weave = np.zeros((4, 2 * LANES, 2 * LANES), np.float32)
    for t in range(4):
        for upper in range(2):
            for lane in range(LANES):
                c = 4 * upper + (lane // 32 - t) % 4
                weave[t, upper * LANES + lane, 8 * (lane % 32) + c] = 1.0
    return twiddle, main, weave.astype(ml_dtypes.bfloat16)


LIGHT = pl.CostEstimate(flops=0, bytes_accessed=0, transcendentals=0)


def compiler_params():
    return pltpu.CompilerParams(vmem_limit_bytes=VMEM)


def store_lanes(out, value, half):
    if half == 0:
        out[...] = value
    else:
        out[...] = jnp.zeros(out.shape, out.dtype)
        out[..., : ROWS - LANES] = value


PARTNERS = ((0, 0), (0, 1), (1, 0), (1, 1))


def pack(place, fields, field, after):
    def kernel(place, a, *refs):
        outs = refs[len(after) :]
        if field == 0:
            for hi in range(2):
                for core in range(2):
                    outs[0][hi, :, core, 0] = a[hi, :, core, 0, :, :LANES]
                    store_lanes(outs[0].at[hi, :, core, 1], a[hi, :, core, 0, :, LANES:], 1)
        for half in range(2 * field):
            for i, (dh, dc) in enumerate(PARTNERS):
                to_hi = pl.ds(lax.rem(place[0] + dh, 2), 1)
                to_core = lax.rem(place[2] + dc, 2)
                lanes = slice(0, LANES) if half == 0 else slice(LANES, ROWS)
                for z in range(2):
                    store_lanes(outs[i].at[pl.ds(z, 1)], a[to_hi, z, to_core, 0, :, lanes], half)
            outs = outs[4:]

    parts = 8 * field
    shape = [jax.ShapeDtypeStruct((NZ, STRIP, LANES), jnp.float32)] * parts
    spec = [pl.BlockSpec((2, STRIP, LANES), lambda i, place: (i, 0, 0))] * parts
    if field == 0:
        shape.insert(0, jax.ShapeDtypeStruct((2, NZ, 2, 2, STRIP, LANES), jnp.float32))
        spec.insert(0, pl.BlockSpec((2, 2, 2, 2, STRIP, LANES), lambda i, place: (0, i, 0, 0, 0, 0)))
    return pl.pallas_call(
        kernel,
        grid_spec=pltpu.PrefetchScalarGridSpec(
            num_scalar_prefetch=1,
            grid=(4,),
            in_specs=[pl.BlockSpec((2, 2, 2, 1, STRIP, ROWS), lambda i, place: (0, i, 0, field, 0, 0))]
            + [pl.BlockSpec(memory_space=pl.ANY)] * len(after),
            out_specs=spec,
        ),
        out_shape=shape,
        compiler_params=compiler_params(),
        cost_estimate=LIGHT,
        name="pack",
    )(place, fields, *after)


def pack_z(place, parts, after):
    def kernel(place, *refs):
        sources, outs = refs[:4], refs[-7:]
        for dz in range(1, NZ):
            to_z = lax.rem(place[1] + dz, NZ)
            for i in range(4):
                outs[dz - 1][i] = sources[i][to_z]

    shape = jax.ShapeDtypeStruct((4, STRIP, LANES), jnp.float32)
    anywhere = pl.BlockSpec(memory_space=pl.ANY)
    local = pl.BlockSpec(memory_space=pltpu.VMEM)
    return pl.pallas_call(
        kernel,
        in_specs=[pl.BlockSpec(memory_space=pltpu.SMEM)] + [local] * 4 + [anywhere] * len(after),
        out_specs=[local] * 7,
        out_shape=[shape] * 7,
        compiler_params=compiler_params(),
        cost_estimate=LIGHT,
        name="pack_z",
    )(place, *parts, *after)


def nine_point(v):
    sums = [v[i] + v[9 - i] for i in range(1, 5)]
    differences = [v[i] - v[9 - i] for i in range(1, 5)]
    result = [(v[0] + ((sums[0] + sums[1]) + (sums[2] + sums[3])), None)]
    for m in range(1, 5):
        re, im = v[0], None
        for i in range(1, 5):
            re = re + sums[i - 1] * math.cos(2 * math.pi * i * m / 9)
            if i * m % 9:
                term = differences[i - 1] * -math.sin(2 * math.pi * i * m / 9)
                im = term if im is None else im + term
        result.append((re, im))
    return result


def fold(columns, folded, i, carry):
    at = pl.multiple_of(i * TILE, 8)
    x = []
    for a in range(18):
        tiles = []
        for part in range(TILE // 8):
            tile = 16 * a + 2 * i + part
            tiles.append(columns[lax.div(tile, 9), pl.ds(pl.multiple_of(8 * lax.rem(tile, 9), 8), 8), :])
        x.append(jnp.concatenate(tiles, axis=0))
    pairs = [(x[a], x[a + 9]) if a % 2 == 0 else (x[a + 9], x[a]) for a in range(9)]
    even = nine_point([a + b for a, b in pairs])
    odd = nine_point([a - b for a, b in pairs])
    classes = [(even[0][0], odd[0][0])]
    for c in range(1, NQ):
        if c % 2 == 0:
            classes.append(even[c // 2])
        else:
            re, im = odd[(9 - c) // 2]
            classes.append((re, -im))
    at = pl.multiple_of(i * TILE, TILE)
    for q, values in enumerate(classes):
        for comp, value in enumerate(values):
            rows = pl.ds(LANES * comp + at, TILE)
            high = value.astype(jnp.bfloat16)
            folded[q, rows, :LANES] = high
            folded[q, rows, LANES:] = (value - high.astype(jnp.float32)).astype(jnp.bfloat16)
    return carry


def x_transform(place, pieces, after, weight):
    whole = len(pieces) == 1
    halves = pieces[0].shape[1] if whole else 1

    def kernel(place, *refs):
        sources = refs[: len(pieces)]
        table = refs[len(pieces)]
        out, columns, folded, tables, sems, table_sem = refs[-6:]
        load = pltpu.make_async_copy(table, tables, table_sem)
        copies = [[], []]
        if whole:
            for half in range(halves):
                copies[half].append(pltpu.make_async_copy(sources[0].at[:, half], columns.at[half], sems.at[half]))
        else:
            hi, z, core = place[0], place[1], place[2]
            for i, (dh, dc) in enumerate(PARTNERS):
                from_hi = lax.rem(hi + dh, 2)
                from_core = lax.rem(core + dc, 2)
                for dz in range(NZ):
                    from_z = lax.rem(z + NZ - dz, NZ)
                    source = sources[i].at[z] if dz == 0 else sources[3 + dz].at[i]
                    sender = from_hi * 16 + from_z * 2 + from_core
                    copies[0].append(pltpu.make_async_copy(source, columns.at[0, sender], sems.at[0]))
        for copy in copies[0] + copies[1]:
            copy.start()
        load.start()
        for half in range(halves):
            for copy in copies[half]:
                copy.wait()
            lax.fori_loop(0, LANES // TILE, functools.partial(fold, columns.at[half], folded), 0)
            if half == 0:
                load.wait()
            for q in range(NQ):
                product = jnp.dot(tables[q], folded[q], preferred_element_type=jnp.float32)
                upper, lower = product[:256], product[256:]
                total = upper[:, :LANES] + (upper[:, LANES:] + lower[:, :LANES])
                total = total.reshape(NJ, 2, 2, 8, LANES)
                for group, number in enumerate((0, 9) if q == 0 else (q, 18 - q)):
                    out[:, half, :, number] = total[:, group]

    anywhere = pl.BlockSpec(memory_space=pl.ANY)
    local = pl.BlockSpec(memory_space=pltpu.VMEM)
    shape = (NJ, halves, 2, 18, 8, LANES)
    return pl.pallas_call(
        kernel,
        in_specs=[pl.BlockSpec(memory_space=pltpu.SMEM)] + [anywhere] * (len(pieces) + 1 + len(after)),
        out_specs=local,
        scratch_shapes=[
            pltpu.VMEM((halves, 32, STRIP, LANES), jnp.float32),
            pltpu.VMEM((NQ, 256, 256), jnp.bfloat16),
            pltpu.VMEM((NQ, 512, 256), jnp.bfloat16),
            pltpu.SemaphoreType.DMA((2,)),
            pltpu.SemaphoreType.DMA,
        ],
        out_shape=jax.ShapeDtypeStruct(shape, jnp.float32),
        compiler_params=compiler_params(),
        cost_estimate=pl.CostEstimate(flops=weight, bytes_accessed=0, transcendentals=0),
        name="x_transform",
    )(place, *pieces, jnp.asarray(x_table()), *after)


def eight_point(re, im):
    def add(a, b):
        return a[0] + b[0], a[1] + b[1]

    def sub(a, b):
        return a[0] - b[0], a[1] - b[1]

    def four(v):
        s, d = add(v[0], v[2]), sub(v[0], v[2])
        t, e = add(v[1], v[3]), sub(v[1], v[3])
        turned = e[1], -e[0]
        return add(s, t), add(d, turned), sub(s, t), sub(d, turned)

    values = list(zip(re, im))
    even = four(values[0::2])
    odd = four(values[1::2])
    root = math.sqrt(0.5)
    o1 = (odd[1][0] + odd[1][1]) * root, (odd[1][1] - odd[1][0]) * root
    o2 = odd[2][1], -odd[2][0]
    o3 = (odd[3][1] - odd[3][0]) * root, (odd[3][0] + odd[3][1]) * -root
    odd = odd[0], o1, o2, o3
    return [add(e, o) for e, o in zip(even, odd)] + [sub(e, o) for e, o in zip(even, odd)]


def y_kernel(count, *refs):
    sources = refs[:count]
    twiddle, main, weave = refs[count : count + 3]
    out, gathered, high, low, mixed, woven, sems = refs[-7:]
    copies = []
    for half in range(2):
        source = sources[0].at[:, half] if len(sources) == 1 else sources[half].at[:, 0]
        copies.append(pltpu.make_async_copy(source, gathered.at[half], sems.at[half]))
    for copy in copies:
        copy.start()
    for half in range(2):
        source = gathered.at[half]
        copies[half].wait()

        def fold(i, carry, half=half, source=source):
            rows = pl.ds(pl.multiple_of(i * TILE, TILE), TILE)
            re = [source[j, 0, rows, :] for j in range(NJ)]
            im = [source[j, 1, rows, :] for j in range(NJ)]
            for c, (a, b) in enumerate(eight_point(re, im)):
                if c > 0:
                    cosine = twiddle[half, c, 0:1, :]
                    sine = twiddle[half, c, 1:2, :]
                    a, b = a * cosine + b * sine, b * cosine - a * sine
                for comp, value in enumerate((a, b)):
                    lanes = slice((2 * half + comp) * LANES, (2 * half + comp + 1) * LANES)
                    top = value.astype(jnp.bfloat16)
                    high[c, rows, lanes] = top
                    low[c, rows, lanes] = (value - top.astype(jnp.float32)).astype(jnp.bfloat16)
            return carry

        lax.fori_loop(0, 144 // TILE, fold, 0)

    for c in range(NJ):
        a = high[c]
        value = (
            jnp.dot(a, main[0], preferred_element_type=jnp.float32)
            + jnp.dot(low[c], main[0], preferred_element_type=jnp.float32)
            + jnp.dot(a, main[1], preferred_element_type=jnp.float32)
        )
        for part in range(4):
            piece = value[:, part * LANES : (part + 1) * LANES]
            if c % 4 > 0:
                piece = pltpu.roll(piece, 32 * (c % 4), 1)
            for group in range(18):
                mixed[c, part, pl.ds(group, 8, stride=18), :] = piece[8 * group : 8 * group + 8]

    slot = lax.broadcasted_iota(jnp.int32, (144, LANES), 1) // 32
    for t in range(4):
        for comp in range(2):
            for upper in range(2):
                part = 2 * comp + upper
                for group in range(2):
                    value = mixed[4 * group, part]
                    for c in range(1, 4):
                        value = jnp.where(slot == (c + t) % 4, mixed[4 * group + c, part], value)
                    top = value.astype(jnp.bfloat16)
                    start = part * 144
                    columns = slice(group * LANES, (group + 1) * LANES)
                    woven[start : start + 144, columns] = top
                    woven[start + 576 : start + 720, columns] = (value - top.astype(jnp.float32)).astype(jnp.bfloat16)
        product = jnp.dot(woven[...], weave[t], preferred_element_type=jnp.float32)
        product = product[:576] + product[576:]
        for comp in range(2):
            for upper in range(2):
                tile = 4 * upper + t
                width = min(256, NY - 256 * tile)
                start = (2 * comp + upper) * 144
                out[comp, 0, :, 256 * tile : 256 * tile + width] = product[start : start + 144, :width]


def y_transform(field, arrays, before):
    twiddle, main, weave = y_tables()
    anywhere = pl.BlockSpec(memory_space=pl.ANY)
    local = pl.BlockSpec(memory_space=pltpu.VMEM)
    inputs = [*arrays, jnp.asarray(twiddle), jnp.asarray(main), jnp.asarray(weave)]
    in_specs = [anywhere] * len(arrays) + [local] * 3
    aliases = {}
    if before is not None:
        aliases = {len(inputs): 0}
        inputs.append(before)
        in_specs.append(anywhere)
    return pl.pallas_call(
        functools.partial(y_kernel, len(arrays)),
        grid=(1,),
        in_specs=in_specs,
        out_specs=pl.BlockSpec((2, 1, 144, NY), lambda i: (0, field, 0, 0)),
        out_shape=jax.ShapeDtypeStruct((2, 2, 144, NY), jnp.float32),
        scratch_shapes=[
            pltpu.VMEM((2, NJ, 2, 144, LANES), jnp.float32),
            pltpu.VMEM((NJ, 144, 512), jnp.bfloat16),
            pltpu.VMEM((NJ, 144, 512), jnp.bfloat16),
            pltpu.VMEM((NJ, 4, 144, LANES), jnp.float32),
            pltpu.VMEM((1152, 256), jnp.bfloat16),
            pltpu.SemaphoreType.DMA((2,)),
        ],
        input_output_aliases=aliases,
        compiler_params=compiler_params(),
        cost_estimate=LIGHT,
        name="y_transform",
    )(*inputs)


def shift(dh, dz, dc):
    pairs = []
    for hi in range(2):
        for z in range(NZ):
            for core in range(2):
                to = (hi + dh) % 2 * 16 + (z + dz) % NZ * 2 + (core + dc) % 2
                pairs.append((hi * 16 + z * 2 + core, to))
    return pairs


def over_y(blocks):
    blocks = blocks.reshape(NJ, -1, 2, 144, LANES)
    return lax.all_to_all(blocks, "gy", split_axis=0, concat_axis=0, tiled=True)


def over_xh(parts):
    return parts[:1] + [lax.ppermute(part, "gx", shift(dh, 0, dc)) for (dh, dc), part in zip(PARTNERS[1:], parts[1:])]


def over_z(sends, order):
    return {dz: lax.ppermute(sends[dz - 1], "gx", shift(0, dz, 0)) for dz in order}


def listed(received):
    return [received[dz] for dz in range(1, NZ)]


def body(fields):
    me = lax.axis_index("gx")
    place = jnp.stack([me // 16, me // 2 % NZ, me % 2]).astype(jnp.int32)
    fields = fields.reshape(2, NZ, 2, 2, STRIP, ROWS)
    first = pack(place, fields, 0, [])[0]
    rest = list(pack(place, fields, 1, [first]))
    first = first.reshape(32, 2, STRIP, LANES)
    first = lax.all_to_all(first, "gx", split_axis=0, concat_axis=0, tiled=True)
    parts = [over_xh(rest[:4]), over_xh(rest[4:])]
    sends = [list(pack_z(place, part, [])) for part in parts]
    second = over_z(sends[0], (1, 7, 2, 6))
    first, sends, second = lax.optimization_barrier((first, sends, second))
    x01 = x_transform(place, [first], [], 2 * 10**10)
    x01, sends = lax.optimization_barrier((x01, sends))
    g01 = over_y(x01)
    second |= over_z(sends[0], (4, 3, 5))
    flying = over_z(sends[1], (4, 2, 6))
    third = over_z(sends[1], (3, 5, 1, 7))
    x2 = x_transform(place, parts[0] + listed(second), [], 2 * 10**10)
    x2, flying = lax.optimization_barrier((x2, flying))
    third |= flying
    g01, x2 = lax.optimization_barrier((g01, x2))
    g2 = over_y(x2)
    x3 = x_transform(place, parts[1] + listed(third), [x2], 2 * 10**11)
    g2, x3 = lax.optimization_barrier((g2, x3))
    g3 = over_y(x3)
    result = y_transform(0, [g01], None)
    return y_transform(1, [g2, g3], result)


def solution(mesh):
    in_specs = (P(None, "gx", "gy"),)
    out_specs = P(None, "gx", "gy", None)
    return jax.shard_map(body, mesh=mesh, in_specs=in_specs, out_specs=out_specs, check_vma=False)
```

```python
import functools
import math

import jax
import jax.numpy as jnp
import ml_dtypes
import numpy as np
from jax import lax
from jax.experimental import pallas as pl
from jax.experimental.pallas import tpu as pltpu
from jax.sharding import PartitionSpec as P

NX = 2304
NY = 2000
KX = 1152
NQ = 9
STRIP = 72
LANES = 128
ROWS = 250
NJ = 8
NZ = 8
TILE = 16
VMEM = 63 * 1000 * 1000


def split_table(table):
    high = table.astype(np.float32).astype(ml_dtypes.bfloat16)
    low = (table - high.astype(np.float64)).astype(np.float32).astype(ml_dtypes.bfloat16)
    return high, low


@functools.cache
def x_table():
    b = np.arange(LANES)
    steps = []
    for q in range(NQ):
        groups = np.array([0, 9] if q == 0 else [q, 18 - q])
        k = 144 * np.arange(NJ)[:, None, None] + groups[None, :, None] + 18 * np.arange(8)[None, None, :]
        angle = 2.0 * np.pi / NX * ((k[..., None] * b) % NX)
        cosine, sine = np.cos(angle), np.sin(angle)
        rows = np.zeros((NJ, 2, 2, 8, 2, LANES))
        for group in range(2):
            if q == 0:
                rows[:, group, 0, :, group] = cosine[:, group]
                rows[:, group, 1, :, group] = -sine[:, group]
            else:
                sign = 1 - 2 * group
                rows[:, group, 0, :, 0] = cosine[:, group]
                rows[:, group, 0, :, 1] = sign * sine[:, group]
                rows[:, group, 1, :, 0] = -sine[:, group]
                rows[:, group, 1, :, 1] = sign * cosine[:, group]
        steps.append(np.concatenate(split_table(rows.reshape(256, 256) / math.sqrt(NX))))
    return np.stack(steps)


@functools.cache
def y_tables():
    b = np.arange(2 * LANES)
    twist = 2.0 * np.pi / NY * ((np.arange(NJ)[:, None] * b[None, :]) % NY)
    twiddle = np.stack([np.cos(twist), np.sin(twist)], axis=1)
    twiddle = twiddle.reshape(NJ, 2, 2, LANES).transpose(2, 0, 1, 3).astype(np.float32)
    d = np.arange(2 * LANES)
    angle = 2.0 * np.pi / ROWS * ((b[:, None] * d[None, :]) % ROWS)
    keep = ((b < ROWS)[:, None] & (d < ROWS)[None, :]).astype(np.float64) / math.sqrt(NY)
    cosine, sine = np.cos(angle) * keep, np.sin(angle) * keep
    from_real = np.concatenate([cosine, -sine], axis=1)
    from_imag = np.concatenate([sine, cosine], axis=1)
    rows = np.concatenate([from_real[:LANES], from_imag[:LANES], from_real[LANES:], from_imag[LANES:]], axis=0)
    main = np.stack(split_table(rows))
    weave = np.zeros((4, 2 * LANES, 2 * LANES), np.float32)
    for t in range(4):
        for upper in range(2):
            for lane in range(LANES):
                c = 4 * upper + (lane // 32 - t) % 4
                weave[t, upper * LANES + lane, 8 * (lane % 32) + c] = 1.0
    return twiddle, main, weave.astype(ml_dtypes.bfloat16)


LIGHT = pl.CostEstimate(flops=0, bytes_accessed=0, transcendentals=0)


def compiler_params():
    return pltpu.CompilerParams(vmem_limit_bytes=VMEM)


def store_lanes(out, value, half):
    if half == 0:
        out[...] = value
    else:
        out[...] = jnp.zeros(out.shape, out.dtype)
        out[..., : ROWS - LANES] = value


PARTNERS = ((0, 0), (0, 1), (1, 0), (1, 1))


def pack(place, fields, field, after):
    def kernel(place, a, *refs):
        outs = refs[len(after) :]
        if field == 0:
            for hi in range(2):
                for core in range(2):
                    outs[0][hi, :, core, 0] = a[hi, :, core, 0, :, :LANES]
                    store_lanes(outs[0].at[hi, :, core, 1], a[hi, :, core, 0, :, LANES:], 1)
        for half in range(2 * field):
            for i, (dh, dc) in enumerate(PARTNERS):
                to_hi = pl.ds(lax.rem(place[0] + dh, 2), 1)
                to_core = lax.rem(place[2] + dc, 2)
                lanes = slice(0, LANES) if half == 0 else slice(LANES, ROWS)
                for z in range(4):
                    store_lanes(outs[i].at[pl.ds(z, 1)], a[to_hi, z, to_core, 0, :, lanes], half)
            outs = outs[4:]

    parts = 8 * field
    shape = [jax.ShapeDtypeStruct((NZ, STRIP, LANES), jnp.float32)] * parts
    spec = [pl.BlockSpec((4, STRIP, LANES), lambda i, place: (i, 0, 0))] * parts
    if field == 0:
        shape.insert(0, jax.ShapeDtypeStruct((2, NZ, 2, 2, STRIP, LANES), jnp.float32))
        spec.insert(0, pl.BlockSpec((2, 4, 2, 2, STRIP, LANES), lambda i, place: (0, i, 0, 0, 0, 0)))
    return pl.pallas_call(
        kernel,
        grid_spec=pltpu.PrefetchScalarGridSpec(
            num_scalar_prefetch=1,
            grid=(2,),
            in_specs=[pl.BlockSpec((2, 4, 2, 1, STRIP, ROWS), lambda i, place: (0, i, 0, field, 0, 0))]
            + [pl.BlockSpec(memory_space=pl.ANY)] * len(after),
            out_specs=spec,
        ),
        out_shape=shape,
        compiler_params=compiler_params(),
        cost_estimate=LIGHT,
        name="pack",
    )(place, fields, *after)


def pack_z(place, parts, after):
    def kernel(place, *refs):
        sources, outs = refs[:4], refs[-7:]
        for dz in range(1, NZ):
            to_z = lax.rem(place[1] + dz, NZ)
            for i in range(4):
                outs[dz - 1][i] = sources[i][to_z]

    shape = jax.ShapeDtypeStruct((4, STRIP, LANES), jnp.float32)
    anywhere = pl.BlockSpec(memory_space=pltpu.HBM)
    local = pl.BlockSpec(memory_space=pltpu.VMEM)
    return pl.pallas_call(
        kernel,
        in_specs=[pl.BlockSpec(memory_space=pltpu.SMEM)] + [local] * 4 + [anywhere] * len(after),
        out_specs=[local] * 7,
        out_shape=[shape] * 7,
        compiler_params=compiler_params(),
        cost_estimate=LIGHT,
        name="pack_z",
    )(place, *parts, *after)


def nine_point(v):
    sums = [v[i] + v[9 - i] for i in range(1, 5)]
    differences = [v[i] - v[9 - i] for i in range(1, 5)]
    result = [(v[0] + ((sums[0] + sums[1]) + (sums[2] + sums[3])), None)]
    for m in range(1, 5):
        re, im = v[0], None
        for i in range(1, 5):
            re = re + sums[i - 1] * math.cos(2 * math.pi * i * m / 9)
            if i * m % 9:
                term = differences[i - 1] * -math.sin(2 * math.pi * i * m / 9)
                im = term if im is None else im + term
        result.append((re, im))
    return result


def fold(columns, folded, i, carry):
    at = pl.multiple_of(i * TILE, 8)
    x = []
    for a in range(18):
        tiles = []
        for part in range(TILE // 8):
            tile = 16 * a + 2 * i + part
            tiles.append(columns[lax.div(tile, 9), pl.ds(pl.multiple_of(8 * lax.rem(tile, 9), 8), 8), :])
        x.append(jnp.concatenate(tiles, axis=0))
    pairs = [(x[a], x[a + 9]) if a % 2 == 0 else (x[a + 9], x[a]) for a in range(9)]
    even = nine_point([a + b for a, b in pairs])
    odd = nine_point([a - b for a, b in pairs])
    classes = [(even[0][0], odd[0][0])]
    for c in range(1, NQ):
        if c % 2 == 0:
            classes.append(even[c // 2])
        else:
            re, im = odd[(9 - c) // 2]
            classes.append((re, -im))
    at = pl.multiple_of(i * TILE, TILE)
    for q, values in enumerate(classes):
        for comp, value in enumerate(values):
            rows = pl.ds(LANES * comp + at, TILE)
            high = value.astype(jnp.bfloat16)
            folded[q, rows, :LANES] = high
            folded[q, rows, LANES:] = (value - high.astype(jnp.float32)).astype(jnp.bfloat16)
    return carry


def x_transform(place, pieces, after, weight):
    whole = len(pieces) == 1
    halves = pieces[0].shape[1] if whole else 1

    def kernel(place, *refs):
        sources = refs[: len(pieces)]
        table = refs[len(pieces)]
        result, out, columns, folded, tables, sems, table_sem, out_sem = refs[-8:]
        stores = []
        load = pltpu.make_async_copy(table, tables, table_sem)
        copies = [[], []]
        if whole:
            for half in range(halves):
                copies[half].append(pltpu.make_async_copy(sources[0].at[:, half], columns.at[half], sems.at[half]))
        else:
            hi, z, core = place[0], place[1], place[2]
            for i, (dh, dc) in enumerate(PARTNERS):
                from_hi = lax.rem(hi + dh, 2)
                from_core = lax.rem(core + dc, 2)
                for dz in range(NZ):
                    from_z = lax.rem(z + NZ - dz, NZ)
                    source = sources[i].at[z] if dz == 0 else sources[3 + dz].at[i]
                    sender = from_hi * 16 + from_z * 2 + from_core
                    copies[0].append(pltpu.make_async_copy(source, columns.at[0, sender], sems.at[0]))
        for copy in copies[0] + copies[1]:
            copy.start()
        load.start()
        for half in range(halves):
            for copy in copies[half]:
                copy.wait()
            lax.fori_loop(0, LANES // TILE, functools.partial(fold, columns.at[half], folded), 0)
            if half == 0:
                load.wait()
            for q in range(NQ):
                product = jnp.dot(tables[q], folded[q], preferred_element_type=jnp.float32)
                upper, lower = product[:256], product[256:]
                total = upper[:, :LANES] + (upper[:, LANES:] + lower[:, :LANES])
                total = total.reshape(NJ, 2, 2, 8, LANES)
                for group, number in enumerate((0, 9) if q == 0 else (q, 18 - q)):
                    out[:, half, :, number] = total[:, group]
            stores.append(pltpu.make_async_copy(out.at[:, half], result.at[:, half], out_sem))
            stores[half].start()
        for store in stores:
            store.wait()

    anywhere = pl.BlockSpec(memory_space=pltpu.HBM)
    local = pl.BlockSpec(memory_space=pltpu.VMEM)
    shape = (NJ, halves, 2, 18, 8, LANES)
    return pl.pallas_call(
        kernel,
        in_specs=[pl.BlockSpec(memory_space=pltpu.SMEM)] + [anywhere] * (len(pieces) + 1 + len(after)),
        out_specs=anywhere,
        scratch_shapes=[
            pltpu.VMEM(shape, jnp.float32),
            pltpu.VMEM((halves, 32, STRIP, LANES), jnp.float32),
            pltpu.VMEM((NQ, 256, 256), jnp.bfloat16),
            pltpu.VMEM((NQ, 512, 256), jnp.bfloat16),
            pltpu.SemaphoreType.DMA((2,)),
            pltpu.SemaphoreType.DMA,
            pltpu.SemaphoreType.DMA,
        ],
        out_shape=jax.ShapeDtypeStruct(shape, jnp.float32),
        compiler_params=compiler_params(),
        cost_estimate=pl.CostEstimate(flops=weight, bytes_accessed=0, transcendentals=0),
        name="x_transform",
    )(place, *pieces, jnp.asarray(x_table()), *after)


def eight_point(re, im):
    def add(a, b):
        return a[0] + b[0], a[1] + b[1]

    def sub(a, b):
        return a[0] - b[0], a[1] - b[1]

    def four(v):
        s, d = add(v[0], v[2]), sub(v[0], v[2])
        t, e = add(v[1], v[3]), sub(v[1], v[3])
        turned = e[1], -e[0]
        return add(s, t), add(d, turned), sub(s, t), sub(d, turned)

    values = list(zip(re, im))
    even = four(values[0::2])
    odd = four(values[1::2])
    root = math.sqrt(0.5)
    o1 = (odd[1][0] + odd[1][1]) * root, (odd[1][1] - odd[1][0]) * root
    o2 = odd[2][1], -odd[2][0]
    o3 = (odd[3][1] - odd[3][0]) * root, (odd[3][0] + odd[3][1]) * -root
    odd = odd[0], o1, o2, o3
    return [add(e, o) for e, o in zip(even, odd)] + [sub(e, o) for e, o in zip(even, odd)]


def y_kernel(count, field, *refs):
    sources = refs[:count]
    twiddle, main_hbm, weave_hbm = refs[count : count + 3]
    result, gathered, high, low, mixed, woven, main, weave, out, sems, out_sem = refs[-11:]
    copies = []
    for half in range(2):
        source = sources[0].at[:, half] if len(sources) == 1 else sources[half].at[:, 0]
        copies.append(pltpu.make_async_copy(source, gathered.at[half], sems.at[half]))
    copies.append(pltpu.make_async_copy(main_hbm, main, sems.at[2]))
    copies.append(pltpu.make_async_copy(weave_hbm, weave, sems.at[3]))
    for copy in copies:
        copy.start()
    for half in range(2):
        source = gathered.at[half]
        copies[half].wait()

        def fold(i, carry, half=half, source=source):
            rows = pl.ds(pl.multiple_of(i * TILE, TILE), TILE)
            re = [source[j, 0, rows, :] for j in range(NJ)]
            im = [source[j, 1, rows, :] for j in range(NJ)]
            for c, (a, b) in enumerate(eight_point(re, im)):
                if c > 0:
                    cosine = twiddle[half, c, 0:1, :]
                    sine = twiddle[half, c, 1:2, :]
                    a, b = a * cosine + b * sine, b * cosine - a * sine
                for comp, value in enumerate((a, b)):
                    lanes = slice((2 * half + comp) * LANES, (2 * half + comp + 1) * LANES)
                    top = value.astype(jnp.bfloat16)
                    high[c, rows, lanes] = top
                    low[c, rows, lanes] = (value - top.astype(jnp.float32)).astype(jnp.bfloat16)
            return carry

        lax.fori_loop(0, 144 // TILE, fold, 0)

    copies[2].wait()
    for c in range(NJ):
        a = high[c]
        value = (
            jnp.dot(a, main[0], preferred_element_type=jnp.float32)
            + jnp.dot(low[c], main[0], preferred_element_type=jnp.float32)
            + jnp.dot(a, main[1], preferred_element_type=jnp.float32)
        )
        for part in range(4):
            piece = value[:, part * LANES : (part + 1) * LANES]
            if c % 4 > 0:
                piece = pltpu.roll(piece, 32 * (c % 4), 1)
            for group in range(18):
                mixed[c, part, pl.ds(group, 8, stride=18), :] = piece[8 * group : 8 * group + 8]

    copies[3].wait()
    slot = lax.broadcasted_iota(jnp.int32, (144, LANES), 1) // 32
    stores = []
    for t in range(4):
        for comp in range(2):
            for upper in range(2):
                part = 2 * comp + upper
                for group in range(2):
                    value = mixed[4 * group, part]
                    for c in range(1, 4):
                        value = jnp.where(slot == (c + t) % 4, mixed[4 * group + c, part], value)
                    top = value.astype(jnp.bfloat16)
                    start = part * 144
                    columns = slice(group * LANES, (group + 1) * LANES)
                    woven[start : start + 144, columns] = top
                    woven[start + 576 : start + 720, columns] = (value - top.astype(jnp.float32)).astype(jnp.bfloat16)
        product = jnp.dot(woven[...], weave[t], preferred_element_type=jnp.float32)
        product = product[:576] + product[576:]
        for comp in range(2):
            for upper in range(2):
                tile = 4 * upper + t
                width = min(256, NY - 256 * tile)
                start = (2 * comp + upper) * 144
                lanes = slice(256 * tile, 256 * tile + width)
                out[comp, :, lanes] = product[start : start + 144, :width]
                stores.append(pltpu.make_async_copy(out.at[comp, :, lanes], result.at[comp, field, :, lanes], out_sem))
                stores[-1].start()
    for store in stores:
        store.wait()


def y_transform(field, arrays, before):
    twiddle, main, weave = y_tables()
    anywhere = pl.BlockSpec(memory_space=pltpu.HBM)
    local = pl.BlockSpec(memory_space=pltpu.VMEM)
    inputs = [*arrays, jnp.asarray(twiddle), jnp.asarray(main), jnp.asarray(weave)]
    in_specs = [anywhere] * len(arrays) + [local] + [anywhere] * 2
    aliases = {}
    if before is not None:
        aliases = {len(inputs): 0}
        inputs.append(before)
        in_specs.append(anywhere)
    return pl.pallas_call(
        functools.partial(y_kernel, len(arrays), field),
        in_specs=in_specs,
        out_specs=anywhere,
        out_shape=jax.ShapeDtypeStruct((2, 2, 144, NY), jnp.float32),
        scratch_shapes=[
            pltpu.VMEM((2, NJ, 2, 144, LANES), jnp.float32),
            pltpu.VMEM((NJ, 144, 512), jnp.bfloat16),
            pltpu.VMEM((NJ, 144, 512), jnp.bfloat16),
            pltpu.VMEM((NJ, 4, 144, LANES), jnp.float32),
            pltpu.VMEM((1152, 256), jnp.bfloat16),
            pltpu.VMEM((2, 512, 512), jnp.bfloat16),
            pltpu.VMEM((4, 256, 256), jnp.bfloat16),
            pltpu.VMEM((2, 144, NY), jnp.float32),
            pltpu.SemaphoreType.DMA((4,)),
            pltpu.SemaphoreType.DMA,
        ],
        input_output_aliases=aliases,
        compiler_params=compiler_params(),
        cost_estimate=LIGHT,
        name="y_transform",
    )(*inputs)


def shift(dh, dz, dc):
    pairs = []
    for hi in range(2):
        for z in range(NZ):
            for core in range(2):
                to = (hi + dh) % 2 * 16 + (z + dz) % NZ * 2 + (core + dc) % 2
                pairs.append((hi * 16 + z * 2 + core, to))
    return pairs


def over_y(blocks):
    blocks = blocks.reshape(NJ, -1, 2, 144, LANES)
    return lax.all_to_all(blocks, "gy", split_axis=0, concat_axis=0, tiled=True)


def over_xh(parts):
    return parts[:1] + [lax.ppermute(part, "gx", shift(dh, 0, dc)) for (dh, dc), part in zip(PARTNERS[1:], parts[1:])]


def over_z(sends, order):
    return {dz: lax.ppermute(sends[dz - 1], "gx", shift(0, dz, 0)) for dz in order}


def listed(received):
    return [received[dz] for dz in range(1, NZ)]


def body(fields):
    me = lax.axis_index("gx")
    place = jnp.stack([me // 16, me // 2 % NZ, me % 2]).astype(jnp.int32)
    fields = fields.reshape(2, NZ, 2, 2, STRIP, ROWS)
    first = pack(place, fields, 0, [])[0]
    rest = list(pack(place, fields, 1, [first]))
    first = first.reshape(32, 2, STRIP, LANES)
    first = lax.all_to_all(first, "gx", split_axis=0, concat_axis=0, tiled=True)
    parts = [over_xh(rest[:4]), over_xh(rest[4:])]
    sends = [list(pack_z(place, part, [])) for part in parts]
    second = over_z(sends[0], (1, 7, 2, 6))
    first, sends, second = lax.optimization_barrier((first, sends, second))
    flying = over_z(sends[0], (4,))
    x01 = x_transform(place, [first], [], 2 * 10**10)
    x01, sends, flying = lax.optimization_barrier((x01, sends, flying))
    g01 = over_y(x01)
    second |= flying | over_z(sends[0], (3, 5))
    flying = over_z(sends[1], (4, 2, 6))
    third = over_z(sends[1], (3, 5, 1, 7))
    x2 = x_transform(place, parts[0] + listed(second), [], 2 * 10**10)
    x2, flying = lax.optimization_barrier((x2, flying))
    third |= flying
    g01, x2 = lax.optimization_barrier((g01, x2))
    g2 = over_y(x2)
    x3 = x_transform(place, parts[1] + listed(third), [x2], 2 * 10**11)
    g2, x3 = lax.optimization_barrier((g2, x3))
    g3 = over_y(x3)
    result = y_transform(0, [g01], None)
    return y_transform(1, [g2, g3], result)


def solution(mesh):
    in_specs = (P(None, "gx", "gy"),)
    out_specs = P(None, "gx", "gy", None)
    return jax.shard_map(body, mesh=mesh, in_specs=in_specs, out_specs=out_specs, check_vma=False)
```

```python
import functools
import math

import jax
import jax.numpy as jnp
import ml_dtypes
import numpy as np
from jax import lax
from jax.experimental import pallas as pl
from jax.experimental.pallas import tpu as pltpu
from jax.sharding import PartitionSpec as P

NX = 2304
NY = 2000
KX = 1152
NQ = 9
STRIP = 72
LANES = 128
ROWS = 250
NJ = 8
NZ = 8
TILE = 16
VMEM = 63 * 1000 * 1000


def split_table(table):
    high = table.astype(np.float32).astype(ml_dtypes.bfloat16)
    low = (table - high.astype(np.float64)).astype(np.float32).astype(ml_dtypes.bfloat16)
    return high, low


@functools.cache
def x_table():
    b = np.arange(LANES)
    steps = []
    for q in range(NQ):
        groups = np.array([0, 9] if q == 0 else [q, 18 - q])
        k = 144 * np.arange(NJ)[:, None, None] + groups[None, :, None] + 18 * np.arange(8)[None, None, :]
        angle = 2.0 * np.pi / NX * ((k[..., None] * b) % NX)
        cosine, sine = np.cos(angle), np.sin(angle)
        rows = np.zeros((NJ, 2, 2, 8, 2, LANES))
        for group in range(2):
            if q == 0:
                rows[:, group, 0, :, group] = cosine[:, group]
                rows[:, group, 1, :, group] = -sine[:, group]
            else:
                sign = 1 - 2 * group
                rows[:, group, 0, :, 0] = cosine[:, group]
                rows[:, group, 0, :, 1] = sign * sine[:, group]
                rows[:, group, 1, :, 0] = -sine[:, group]
                rows[:, group, 1, :, 1] = sign * cosine[:, group]
        steps.append(np.concatenate(split_table(rows.reshape(256, 256) / math.sqrt(NX))))
    return np.stack(steps)


@functools.cache
def y_tables():
    b = np.arange(2 * LANES)
    twist = 2.0 * np.pi / NY * ((np.arange(NJ)[:, None] * b[None, :]) % NY)
    twiddle = np.stack([np.cos(twist), np.sin(twist)], axis=1)
    twiddle = twiddle.reshape(NJ, 2, 2, LANES).transpose(2, 0, 1, 3).astype(np.float32)
    d = np.arange(2 * LANES)
    angle = 2.0 * np.pi / ROWS * ((b[:, None] * d[None, :]) % ROWS)
    keep = ((b < ROWS)[:, None] & (d < ROWS)[None, :]).astype(np.float64) / math.sqrt(NY)
    cosine, sine = np.cos(angle) * keep, np.sin(angle) * keep
    from_real = np.concatenate([cosine, -sine], axis=1)
    from_imag = np.concatenate([sine, cosine], axis=1)
    rows = np.concatenate([from_real[:LANES], from_imag[:LANES], from_real[LANES:], from_imag[LANES:]], axis=0)
    main = np.stack(split_table(rows))
    weave = np.zeros((4, 2 * LANES, 2 * LANES), np.float32)
    for t in range(4):
        for upper in range(2):
            for lane in range(LANES):
                c = 4 * upper + (lane // 32 - t) % 4
                weave[t, upper * LANES + lane, 8 * (lane % 32) + c] = 1.0
    return twiddle, main, weave.astype(ml_dtypes.bfloat16)


LIGHT = pl.CostEstimate(flops=0, bytes_accessed=0, transcendentals=0)


def compiler_params():
    return pltpu.CompilerParams(vmem_limit_bytes=VMEM)


def store_lanes(out, value, half):
    if half == 0:
        out[...] = value
    else:
        out[...] = jnp.zeros(out.shape, out.dtype)
        out[..., : ROWS - LANES] = value


PARTNERS = ((0, 0), (0, 1), (1, 0), (1, 1))


def pack(place, fields, field, after):
    def kernel(place, a, *refs):
        outs = refs[len(after) :]
        if field == 0:
            for hi in range(2):
                for core in range(2):
                    outs[0][hi, :, core, 0] = a[hi, :, core, 0, :, :LANES]
                    store_lanes(outs[0].at[hi, :, core, 1], a[hi, :, core, 0, :, LANES:], 1)
        for half in range(2 * field):
            for i, (dh, dc) in enumerate(PARTNERS):
                to_hi = pl.ds(lax.rem(place[0] + dh, 2), 1)
                to_core = lax.rem(place[2] + dc, 2)
                lanes = slice(0, LANES) if half == 0 else slice(LANES, ROWS)
                for z in range(4):
                    store_lanes(outs[i].at[pl.ds(z, 1)], a[to_hi, z, to_core, 0, :, lanes], half)
            outs = outs[4:]

    parts = 8 * field
    shape = [jax.ShapeDtypeStruct((NZ, STRIP, LANES), jnp.float32)] * parts
    spec = [pl.BlockSpec((4, STRIP, LANES), lambda i, place: (i, 0, 0))] * parts
    if field == 0:
        shape.insert(0, jax.ShapeDtypeStruct((2, NZ, 2, 2, STRIP, LANES), jnp.float32))
        spec.insert(0, pl.BlockSpec((2, 4, 2, 2, STRIP, LANES), lambda i, place: (0, i, 0, 0, 0, 0)))
    return pl.pallas_call(
        kernel,
        grid_spec=pltpu.PrefetchScalarGridSpec(
            num_scalar_prefetch=1,
            grid=(2,),
            in_specs=[pl.BlockSpec((2, 4, 2, 1, STRIP, ROWS), lambda i, place: (0, i, 0, field, 0, 0))]
            + [pl.BlockSpec(memory_space=pl.ANY)] * len(after),
            out_specs=spec,
        ),
        out_shape=shape,
        compiler_params=compiler_params(),
        cost_estimate=LIGHT,
        name="pack",
    )(place, fields, *after)


def pack_z(place, parts, after):
    def kernel(place, *refs):
        sources, outs = refs[:4], refs[-7:]
        for dz in range(1, NZ):
            to_z = lax.rem(place[1] + dz, NZ)
            for i in range(4):
                outs[dz - 1][i] = sources[i][to_z]

    shape = jax.ShapeDtypeStruct((4, STRIP, LANES), jnp.float32)
    anywhere = pl.BlockSpec(memory_space=pltpu.HBM)
    local = pl.BlockSpec(memory_space=pltpu.VMEM)
    return pl.pallas_call(
        kernel,
        in_specs=[pl.BlockSpec(memory_space=pltpu.SMEM)] + [local] * 4 + [anywhere] * len(after),
        out_specs=[local] * 7,
        out_shape=[shape] * 7,
        compiler_params=compiler_params(),
        cost_estimate=LIGHT,
        name="pack_z",
    )(place, *parts, *after)


def nine_point(v):
    sums = [v[i] + v[9 - i] for i in range(1, 5)]
    differences = [v[i] - v[9 - i] for i in range(1, 5)]
    result = [(v[0] + ((sums[0] + sums[1]) + (sums[2] + sums[3])), None)]
    for m in range(1, 5):
        re, im = v[0], None
        for i in range(1, 5):
            re = re + sums[i - 1] * math.cos(2 * math.pi * i * m / 9)
            if i * m % 9:
                term = differences[i - 1] * -math.sin(2 * math.pi * i * m / 9)
                im = term if im is None else im + term
        result.append((re, im))
    return result


def fold(columns, folded, i, carry):
    at = pl.multiple_of(i * TILE, 8)
    x = []
    for a in range(18):
        tiles = []
        for part in range(TILE // 8):
            tile = 16 * a + 2 * i + part
            tiles.append(columns[lax.div(tile, 9), pl.ds(pl.multiple_of(8 * lax.rem(tile, 9), 8), 8), :])
        x.append(jnp.concatenate(tiles, axis=0))
    pairs = [(x[a], x[a + 9]) if a % 2 == 0 else (x[a + 9], x[a]) for a in range(9)]
    even = nine_point([a + b for a, b in pairs])
    odd = nine_point([a - b for a, b in pairs])
    classes = [(even[0][0], odd[0][0])]
    for c in range(1, NQ):
        if c % 2 == 0:
            classes.append(even[c // 2])
        else:
            re, im = odd[(9 - c) // 2]
            classes.append((re, -im))
    at = pl.multiple_of(i * TILE, TILE)
    for q, values in enumerate(classes):
        for comp, value in enumerate(values):
            rows = pl.ds(LANES * comp + at, TILE)
            high = value.astype(jnp.bfloat16)
            folded[q, rows, :LANES] = high
            folded[q, rows, LANES:] = (value - high.astype(jnp.float32)).astype(jnp.bfloat16)
    return carry


def x_transform(place, pieces, after, weight):
    whole = len(pieces) == 1
    halves = pieces[0].shape[1] if whole else 1

    def kernel(place, *refs):
        sources = refs[: len(pieces)]
        table = refs[len(pieces)]
        result, out, columns, folded, tables, sems, table_sem, out_sem = refs[-8:]
        stores = []
        load = pltpu.make_async_copy(table, tables, table_sem)
        copies = [[], []]
        if whole:
            for half in range(halves):
                copies[half].append(pltpu.make_async_copy(sources[0].at[:, half], columns.at[half], sems.at[half]))
        else:
            hi, z, core = place[0], place[1], place[2]
            for i, (dh, dc) in enumerate(PARTNERS):
                from_hi = lax.rem(hi + dh, 2)
                from_core = lax.rem(core + dc, 2)
                for dz in range(NZ):
                    from_z = lax.rem(z + NZ - dz, NZ)
                    source = sources[i].at[z] if dz == 0 else sources[3 + dz].at[i]
                    sender = from_hi * 16 + from_z * 2 + from_core
                    copies[0].append(pltpu.make_async_copy(source, columns.at[0, sender], sems.at[0]))
        for copy in copies[0] + copies[1]:
            copy.start()
        load.start()
        for half in range(halves):
            for copy in copies[half]:
                copy.wait()
            lax.fori_loop(0, LANES // TILE, functools.partial(fold, columns.at[half], folded), 0)
            if half == 0:
                load.wait()
            for q in range(NQ):
                product = jnp.dot(tables[q], folded[q], preferred_element_type=jnp.float32)
                upper, lower = product[:256], product[256:]
                total = upper[:, :LANES] + (upper[:, LANES:] + lower[:, :LANES])
                total = total.reshape(NJ, 2, 2, 8, LANES)
                for group, number in enumerate((0, 9) if q == 0 else (q, 18 - q)):
                    out[:, half, :, number] = total[:, group]
            stores.append(pltpu.make_async_copy(out.at[:, half], result.at[:, half], out_sem))
            stores[half].start()
        for store in stores:
            store.wait()

    anywhere = pl.BlockSpec(memory_space=pltpu.HBM)
    local = pl.BlockSpec(memory_space=pltpu.VMEM)
    shape = (NJ, halves, 2, 18, 8, LANES)
    return pl.pallas_call(
        kernel,
        in_specs=[pl.BlockSpec(memory_space=pltpu.SMEM)] + [anywhere] * (len(pieces) + 1 + len(after)),
        out_specs=anywhere,
        scratch_shapes=[
            pltpu.VMEM(shape, jnp.float32),
            pltpu.VMEM((halves, 32, STRIP, LANES), jnp.float32),
            pltpu.VMEM((NQ, 256, 256), jnp.bfloat16),
            pltpu.VMEM((NQ, 512, 256), jnp.bfloat16),
            pltpu.SemaphoreType.DMA((2,)),
            pltpu.SemaphoreType.DMA,
            pltpu.SemaphoreType.DMA,
        ],
        out_shape=jax.ShapeDtypeStruct(shape, jnp.float32),
        compiler_params=compiler_params(),
        cost_estimate=pl.CostEstimate(flops=weight, bytes_accessed=0, transcendentals=0),
        name="x_transform",
    )(place, *pieces, jnp.asarray(x_table()), *after)


def eight_point(re, im):
    def add(a, b):
        return a[0] + b[0], a[1] + b[1]

    def sub(a, b):
        return a[0] - b[0], a[1] - b[1]

    def four(v):
        s, d = add(v[0], v[2]), sub(v[0], v[2])
        t, e = add(v[1], v[3]), sub(v[1], v[3])
        turned = e[1], -e[0]
        return add(s, t), add(d, turned), sub(s, t), sub(d, turned)

    values = list(zip(re, im))
    even = four(values[0::2])
    odd = four(values[1::2])
    root = math.sqrt(0.5)
    o1 = (odd[1][0] + odd[1][1]) * root, (odd[1][1] - odd[1][0]) * root
    o2 = odd[2][1], -odd[2][0]
    o3 = (odd[3][1] - odd[3][0]) * root, (odd[3][0] + odd[3][1]) * -root
    odd = odd[0], o1, o2, o3
    return [add(e, o) for e, o in zip(even, odd)] + [sub(e, o) for e, o in zip(even, odd)]


def y_kernel(count, field, *refs):
    sources = refs[:count]
    twiddle, main_hbm, weave_hbm = refs[count : count + 3]
    result, gathered, high, low, mixed, woven, main, weave, out, sems, out_sem = refs[-11:]
    copies = []
    for half in range(2):
        source = sources[0].at[:, half] if len(sources) == 1 else sources[half].at[:, 0]
        copies.append(pltpu.make_async_copy(source, gathered.at[half], sems.at[half]))
    copies.append(pltpu.make_async_copy(main_hbm, main, sems.at[2]))
    copies.append(pltpu.make_async_copy(weave_hbm, weave, sems.at[3]))
    for copy in copies:
        copy.start()
    for half in range(2):
        source = gathered.at[half]
        copies[half].wait()

        def fold(i, carry, half=half, source=source):
            rows = pl.ds(pl.multiple_of(i * TILE, TILE), TILE)
            re = [source[j, 0, rows, :] for j in range(NJ)]
            im = [source[j, 1, rows, :] for j in range(NJ)]
            for c, (a, b) in enumerate(eight_point(re, im)):
                if c > 0:
                    cosine = twiddle[half, c, 0:1, :]
                    sine = twiddle[half, c, 1:2, :]
                    a, b = a * cosine + b * sine, b * cosine - a * sine
                for comp, value in enumerate((a, b)):
                    lanes = slice((2 * half + comp) * LANES, (2 * half + comp + 1) * LANES)
                    top = value.astype(jnp.bfloat16)
                    high[c, rows, lanes] = top
                    low[c, rows, lanes] = (value - top.astype(jnp.float32)).astype(jnp.bfloat16)
            return carry

        lax.fori_loop(0, 144 // TILE, fold, 0)

    copies[2].wait()
    for c in range(NJ):
        a = high[c]
        value = (
            jnp.dot(a, main[0], preferred_element_type=jnp.float32)
            + jnp.dot(low[c], main[0], preferred_element_type=jnp.float32)
            + jnp.dot(a, main[1], preferred_element_type=jnp.float32)
        )
        for part in range(4):
            piece = value[:, part * LANES : (part + 1) * LANES]
            if c % 4 > 0:
                piece = pltpu.roll(piece, 32 * (c % 4), 1)
            for group in range(18):
                mixed[c, part, pl.ds(group, 8, stride=18), :] = piece[8 * group : 8 * group + 8]

    copies[3].wait()
    slot = lax.broadcasted_iota(jnp.int32, (144, LANES), 1) // 32
    stores = []
    for t in range(4):
        for comp in range(2):
            for upper in range(2):
                part = 2 * comp + upper
                for group in range(2):
                    value = mixed[4 * group, part]
                    for c in range(1, 4):
                        value = jnp.where(slot == (c + t) % 4, mixed[4 * group + c, part], value)
                    top = value.astype(jnp.bfloat16)
                    start = part * 144
                    columns = slice(group * LANES, (group + 1) * LANES)
                    woven[start : start + 144, columns] = top
                    woven[start + 576 : start + 720, columns] = (value - top.astype(jnp.float32)).astype(jnp.bfloat16)
        product = jnp.dot(woven[...], weave[t], preferred_element_type=jnp.float32)
        product = product[:576] + product[576:]
        for comp in range(2):
            for upper in range(2):
                tile = 4 * upper + t
                width = min(256, NY - 256 * tile)
                start = (2 * comp + upper) * 144
                lanes = slice(256 * tile, 256 * tile + width)
                out[comp, :, lanes] = product[start : start + 144, :width]
                stores.append(pltpu.make_async_copy(out.at[comp, :, lanes], result.at[comp, field, :, lanes], out_sem))
                stores[-1].start()
    for store in stores:
        store.wait()


def y_transform(field, arrays, before):
    twiddle, main, weave = y_tables()
    anywhere = pl.BlockSpec(memory_space=pltpu.HBM)
    local = pl.BlockSpec(memory_space=pltpu.VMEM)
    inputs = [*arrays, jnp.asarray(twiddle), jnp.asarray(main), jnp.asarray(weave)]
    in_specs = [anywhere] * len(arrays) + [local] + [anywhere] * 2
    aliases = {}
    if before is not None:
        aliases = {len(inputs): 0}
        inputs.append(before)
        in_specs.append(anywhere)
    return pl.pallas_call(
        functools.partial(y_kernel, len(arrays), field),
        in_specs=in_specs,
        out_specs=anywhere,
        out_shape=jax.ShapeDtypeStruct((2, 2, 144, NY), jnp.float32),
        scratch_shapes=[
            pltpu.VMEM((2, NJ, 2, 144, LANES), jnp.float32),
            pltpu.VMEM((NJ, 144, 512), jnp.bfloat16),
            pltpu.VMEM((NJ, 144, 512), jnp.bfloat16),
            pltpu.VMEM((NJ, 4, 144, LANES), jnp.float32),
            pltpu.VMEM((1152, 256), jnp.bfloat16),
            pltpu.VMEM((2, 512, 512), jnp.bfloat16),
            pltpu.VMEM((4, 256, 256), jnp.bfloat16),
            pltpu.VMEM((2, 144, NY), jnp.float32),
            pltpu.SemaphoreType.DMA((4,)),
            pltpu.SemaphoreType.DMA,
        ],
        input_output_aliases=aliases,
        compiler_params=compiler_params(),
        cost_estimate=LIGHT,
        name="y_transform",
    )(*inputs)


def shift(dh, dz, dc):
    pairs = []
    for hi in range(2):
        for z in range(NZ):
            for core in range(2):
                to = (hi + dh) % 2 * 16 + (z + dz) % NZ * 2 + (core + dc) % 2
                pairs.append((hi * 16 + z * 2 + core, to))
    return pairs


def over_y(blocks):
    blocks = blocks.reshape(NJ, -1, 2, 144, LANES)
    return lax.all_to_all(blocks, "gy", split_axis=0, concat_axis=0, tiled=True)


def over_xh(parts):
    return parts[:1] + [lax.ppermute(part, "gx", shift(dh, 0, dc)) for (dh, dc), part in zip(PARTNERS[1:], parts[1:])]


def over_z(sends, order):
    return {dz: lax.ppermute(sends[dz - 1], "gx", shift(0, dz, 0)) for dz in order}


def listed(received):
    return [received[dz] for dz in range(1, NZ)]


def body(fields):
    me = lax.axis_index("gx")
    place = jnp.stack([me // 16, me // 2 % NZ, me % 2]).astype(jnp.int32)
    fields = fields.reshape(2, NZ, 2, 2, STRIP, ROWS)
    first = pack(jnp.zeros(3, jnp.int32), fields, 0, [])[0]
    rest = list(pack(place, fields, 1, [first]))
    first = first.reshape(32, 2, STRIP, LANES)
    first = lax.all_to_all(first, "gx", split_axis=0, concat_axis=0, tiled=True)
    parts = [over_xh(rest[:4]), over_xh(rest[4:])]
    sends = [list(pack_z(place, part, [])) for part in parts]
    second = over_z(sends[0], (1, 7, 2, 6))
    first, sends, second = lax.optimization_barrier((first, sends, second))
    flying = over_z(sends[0], (4,))
    x01 = x_transform(place, [first], [], 2 * 10**10)
    x01, sends, flying = lax.optimization_barrier((x01, sends, flying))
    g01 = over_y(x01)
    second |= flying | over_z(sends[0], (3, 5))
    flying = over_z(sends[1], (4, 2, 6))
    third = over_z(sends[1], (3, 5, 1, 7))
    x2 = x_transform(place, parts[0] + listed(second), [], 2 * 10**10)
    x2, flying = lax.optimization_barrier((x2, flying))
    third |= flying
    g01, x2 = lax.optimization_barrier((g01, x2))
    g2 = over_y(x2)
    x3 = x_transform(place, parts[1] + listed(third), [x2], 2 * 10**11)
    g2, x3 = lax.optimization_barrier((g2, x3))
    g3 = over_y(x3)
    result = y_transform(0, [g01], None)
    return y_transform(1, [g2, g3], result)


def solution(mesh):
    in_specs = (P(None, "gx", "gy"),)
    out_specs = P(None, "gx", "gy", None)
    return jax.shard_map(body, mesh=mesh, in_specs=in_specs, out_specs=out_specs, check_vma=False)
```

```python
import functools
import math

import jax
import jax.numpy as jnp
import ml_dtypes
import numpy as np
from jax import lax
from jax.experimental import pallas as pl
from jax.experimental.pallas import tpu as pltpu
from jax.sharding import PartitionSpec as P

NX = 2304
NY = 2000
KX = 1152
NQ = 9
STRIP = 72
LANES = 128
ROWS = 250
NJ = 8
NZ = 8
TILE = 16
VMEM = 63 * 1000 * 1000


def split_table(table):
    high = table.astype(np.float32).astype(ml_dtypes.bfloat16)
    low = (table - high.astype(np.float64)).astype(np.float32).astype(ml_dtypes.bfloat16)
    return high, low


@functools.cache
def x_table():
    b = np.arange(LANES)
    steps = []
    for q in range(NQ):
        groups = np.array([0, 9] if q == 0 else [q, 18 - q])
        k = 144 * np.arange(NJ)[:, None, None] + groups[None, :, None] + 18 * np.arange(8)[None, None, :]
        angle = 2.0 * np.pi / NX * ((k[..., None] * b) % NX)
        cosine, sine = np.cos(angle), np.sin(angle)
        rows = np.zeros((NJ, 2, 2, 8, 2, LANES))
        for group in range(2):
            if q == 0:
                rows[:, group, 0, :, group] = cosine[:, group]
                rows[:, group, 1, :, group] = -sine[:, group]
            else:
                sign = 1 - 2 * group
                rows[:, group, 0, :, 0] = cosine[:, group]
                rows[:, group, 0, :, 1] = sign * sine[:, group]
                rows[:, group, 1, :, 0] = -sine[:, group]
                rows[:, group, 1, :, 1] = sign * cosine[:, group]
        steps.append(np.concatenate(split_table(rows.reshape(256, 256) / math.sqrt(NX))))
    return np.stack(steps)


@functools.cache
def y_tables():
    b = np.arange(2 * LANES)
    twist = 2.0 * np.pi / NY * ((np.arange(NJ)[:, None] * b[None, :]) % NY)
    twiddle = np.stack([np.cos(twist), np.sin(twist)], axis=1)
    twiddle = twiddle.reshape(NJ, 2, 2, LANES).transpose(2, 0, 1, 3).astype(np.float32)
    d = np.arange(2 * LANES)
    angle = 2.0 * np.pi / ROWS * ((b[:, None] * d[None, :]) % ROWS)
    keep = ((b < ROWS)[:, None] & (d < ROWS)[None, :]).astype(np.float64) / math.sqrt(NY)
    cosine, sine = np.cos(angle) * keep, np.sin(angle) * keep
    from_real = np.concatenate([cosine, -sine], axis=1)
    from_imag = np.concatenate([sine, cosine], axis=1)
    rows = np.concatenate([from_real[:LANES], from_imag[:LANES], from_real[LANES:], from_imag[LANES:]], axis=0)
    main = np.stack(split_table(rows))
    weave = np.zeros((4, 2 * LANES, 2 * LANES), np.float32)
    for t in range(4):
        for upper in range(2):
            for lane in range(LANES):
                c = 4 * upper + (lane // 32 - t) % 4
                weave[t, upper * LANES + lane, 8 * (lane % 32) + c] = 1.0
    return twiddle, main, weave.astype(ml_dtypes.bfloat16)


LIGHT = pl.CostEstimate(flops=0, bytes_accessed=0, transcendentals=0)


def compiler_params():
    return pltpu.CompilerParams(vmem_limit_bytes=VMEM)


def store_lanes(out, value, half):
    if half == 0:
        out[...] = value
    else:
        out[...] = jnp.zeros(out.shape, out.dtype)
        out[..., : ROWS - LANES] = value


PARTNERS = ((0, 0), (0, 1), (1, 0), (1, 1))


def pack(place, fields, field, after):
    def kernel(place, a, *refs):
        outs = refs[len(after) :]
        if field == 0:
            for hi in range(2):
                for core in range(2):
                    outs[0][hi, :, core, 0] = a[hi, :, core, 0, :, :LANES]
                    store_lanes(outs[0].at[hi, :, core, 1], a[hi, :, core, 0, :, LANES:], 1)
        for half in range(2 * field):
            for i, (dh, dc) in enumerate(PARTNERS):
                to_hi = pl.ds(lax.rem(place[0] + dh, 2), 1)
                to_core = lax.rem(place[2] + dc, 2)
                lanes = slice(0, LANES) if half == 0 else slice(LANES, ROWS)
                for z in range(4):
                    store_lanes(outs[i].at[pl.ds(z, 1)], a[to_hi, z, to_core, 0, :, lanes], half)
            outs = outs[4:]

    parts = 8 * field
    shape = [jax.ShapeDtypeStruct((NZ, STRIP, LANES), jnp.float32)] * parts
    spec = [pl.BlockSpec((4, STRIP, LANES), lambda i, place: (i, 0, 0))] * parts
    if field == 0:
        shape.insert(0, jax.ShapeDtypeStruct((2, NZ, 2, 2, STRIP, LANES), jnp.float32))
        spec.insert(0, pl.BlockSpec((2, 4, 2, 2, STRIP, LANES), lambda i, place: (0, i, 0, 0, 0, 0)))
    return pl.pallas_call(
        kernel,
        grid_spec=pltpu.PrefetchScalarGridSpec(
            num_scalar_prefetch=1,
            grid=(2,),
            in_specs=[pl.BlockSpec((2, 4, 2, 1, STRIP, ROWS), lambda i, place: (0, i, 0, field, 0, 0))]
            + [pl.BlockSpec(memory_space=pl.ANY)] * len(after),
            out_specs=spec,
        ),
        out_shape=shape,
        compiler_params=compiler_params(),
        cost_estimate=LIGHT,
        name="pack",
    )(place, fields, *after)


def pack_z(place, parts, after):
    def kernel(place, *refs):
        sources, outs = refs[:4], refs[-7:]
        for dz in range(1, NZ):
            to_z = lax.rem(place[1] + dz, NZ)
            for i in range(4):
                outs[dz - 1][i] = sources[i][to_z]

    shape = jax.ShapeDtypeStruct((4, STRIP, LANES), jnp.float32)
    anywhere = pl.BlockSpec(memory_space=pltpu.HBM)
    local = pl.BlockSpec(memory_space=pltpu.VMEM)
    return pl.pallas_call(
        kernel,
        in_specs=[pl.BlockSpec(memory_space=pltpu.SMEM)] + [local] * 4 + [anywhere] * len(after),
        out_specs=[local] * 7,
        out_shape=[shape] * 7,
        compiler_params=compiler_params(),
        cost_estimate=LIGHT,
        name="pack_z",
    )(place, *parts, *after)


def nine_point(v):
    sums = [v[i] + v[9 - i] for i in range(1, 5)]
    differences = [v[i] - v[9 - i] for i in range(1, 5)]
    result = [(v[0] + ((sums[0] + sums[1]) + (sums[2] + sums[3])), None)]
    for m in range(1, 5):
        re, im = v[0], None
        for i in range(1, 5):
            re = re + sums[i - 1] * math.cos(2 * math.pi * i * m / 9)
            if i * m % 9:
                term = differences[i - 1] * -math.sin(2 * math.pi * i * m / 9)
                im = term if im is None else im + term
        result.append((re, im))
    return result


def fold(columns, folded, i, carry):
    at = pl.multiple_of(i * TILE, 8)
    x = []
    for a in range(18):
        tiles = []
        for part in range(TILE // 8):
            tile = 16 * a + 2 * i + part
            tiles.append(columns[lax.div(tile, 9), pl.ds(pl.multiple_of(8 * lax.rem(tile, 9), 8), 8), :])
        x.append(jnp.concatenate(tiles, axis=0))
    pairs = [(x[a], x[a + 9]) if a % 2 == 0 else (x[a + 9], x[a]) for a in range(9)]
    even = nine_point([a + b for a, b in pairs])
    odd = nine_point([a - b for a, b in pairs])
    classes = [(even[0][0], odd[0][0])]
    for c in range(1, NQ):
        if c % 2 == 0:
            classes.append(even[c // 2])
        else:
            re, im = odd[(9 - c) // 2]
            classes.append((re, -im))
    at = pl.multiple_of(i * TILE, TILE)
    for q, values in enumerate(classes):
        for comp, value in enumerate(values):
            rows = pl.ds(LANES * comp + at, TILE)
            high = value.astype(jnp.bfloat16)
            folded[q, rows, :LANES] = high
            folded[q, rows, LANES:] = (value - high.astype(jnp.float32)).astype(jnp.bfloat16)
    return carry


def x_transform(place, pieces, after, weight):
    whole = len(pieces) == 1
    halves = pieces[0].shape[1] if whole else 1

    def kernel(place, *refs):
        sources = refs[: len(pieces)]
        table = refs[len(pieces)]
        result, out, columns, folded, tables, sems, table_sem, out_sem = refs[-8:]
        stores = []
        load = pltpu.make_async_copy(table, tables, table_sem)
        copies = [[], []]
        if whole:
            for half in range(halves):
                copies[half].append(pltpu.make_async_copy(sources[0].at[:, half], columns.at[half], sems.at[half]))
        else:
            hi, z, core = place[0], place[1], place[2]
            for i, (dh, dc) in enumerate(PARTNERS):
                from_hi = lax.rem(hi + dh, 2)
                from_core = lax.rem(core + dc, 2)
                for dz in range(NZ):
                    from_z = lax.rem(z + NZ - dz, NZ)
                    source = sources[i].at[z] if dz == 0 else sources[3 + dz].at[i]
                    sender = from_hi * 16 + from_z * 2 + from_core
                    copies[0].append(pltpu.make_async_copy(source, columns.at[0, sender], sems.at[0]))
        for copy in copies[0] + copies[1]:
            copy.start()
        load.start()
        for half in range(halves):
            for copy in copies[half]:
                copy.wait()
            lax.fori_loop(0, LANES // TILE, functools.partial(fold, columns.at[half], folded), 0)
            if half == 0:
                load.wait()
            for q in range(NQ):
                product = jnp.dot(tables[q], folded[q], preferred_element_type=jnp.float32)
                upper, lower = product[:256], product[256:]
                total = upper[:, :LANES] + (upper[:, LANES:] + lower[:, :LANES])
                total = total.reshape(NJ, 2, 2, 8, LANES)
                for group, number in enumerate((0, 9) if q == 0 else (q, 18 - q)):
                    out[:, half, :, number] = total[:, group]
                ready = {4: ((0, 5), (14, 4)), 8: ((5, 9),)}.get(q, ())
                for low, count in ready:
                    classes = pl.ds(low, count)
                    stores.append(
                        pltpu.make_async_copy(out.at[:, half, :, classes], result.at[:, half, :, classes], out_sem)
                    )
                    stores[-1].start()
        for store in stores:
            store.wait()

    anywhere = pl.BlockSpec(memory_space=pltpu.HBM)
    local = pl.BlockSpec(memory_space=pltpu.VMEM)
    shape = (NJ, halves, 2, 18, 8, LANES)
    return pl.pallas_call(
        kernel,
        in_specs=[pl.BlockSpec(memory_space=pltpu.SMEM)] + [anywhere] * (len(pieces) + 1 + len(after)),
        out_specs=anywhere,
        scratch_shapes=[
            pltpu.VMEM(shape, jnp.float32),
            pltpu.VMEM((halves, 32, STRIP, LANES), jnp.float32),
            pltpu.VMEM((NQ, 256, 256), jnp.bfloat16),
            pltpu.VMEM((NQ, 512, 256), jnp.bfloat16),
            pltpu.SemaphoreType.DMA((2,)),
            pltpu.SemaphoreType.DMA,
            pltpu.SemaphoreType.DMA,
        ],
        out_shape=jax.ShapeDtypeStruct(shape, jnp.float32),
        compiler_params=compiler_params(),
        cost_estimate=pl.CostEstimate(flops=weight, bytes_accessed=0, transcendentals=0),
        name="x_transform",
    )(place, *pieces, jnp.asarray(x_table()), *after)


def eight_point(re, im):
    def add(a, b):
        return a[0] + b[0], a[1] + b[1]

    def sub(a, b):
        return a[0] - b[0], a[1] - b[1]

    def four(v):
        s, d = add(v[0], v[2]), sub(v[0], v[2])
        t, e = add(v[1], v[3]), sub(v[1], v[3])
        turned = e[1], -e[0]
        return add(s, t), add(d, turned), sub(s, t), sub(d, turned)

    values = list(zip(re, im))
    even = four(values[0::2])
    odd = four(values[1::2])
    root = math.sqrt(0.5)
    o1 = (odd[1][0] + odd[1][1]) * root, (odd[1][1] - odd[1][0]) * root
    o2 = odd[2][1], -odd[2][0]
    o3 = (odd[3][1] - odd[3][0]) * root, (odd[3][0] + odd[3][1]) * -root
    odd = odd[0], o1, o2, o3
    return [add(e, o) for e, o in zip(even, odd)] + [sub(e, o) for e, o in zip(even, odd)]


def y_kernel(count, field, *refs):
    sources = refs[:count]
    twiddle, main_hbm, weave_hbm = refs[count : count + 3]
    result, gathered, high, low, mixed, woven, main, weave, out, sems, out_sem = refs[-11:]
    copies = []
    for half in range(2):
        source = sources[0].at[:, half] if len(sources) == 1 else sources[half].at[:, 0]
        copies.append(pltpu.make_async_copy(source, gathered.at[half], sems.at[half]))
    copies.append(pltpu.make_async_copy(main_hbm, main, sems.at[2]))
    copies.append(pltpu.make_async_copy(weave_hbm, weave, sems.at[3]))
    for copy in copies:
        copy.start()
    for half in range(2):
        source = gathered.at[half]
        copies[half].wait()

        def fold(i, carry, half=half, source=source):
            rows = pl.ds(pl.multiple_of(i * TILE, TILE), TILE)
            re = [source[j, 0, rows, :] for j in range(NJ)]
            im = [source[j, 1, rows, :] for j in range(NJ)]
            for c, (a, b) in enumerate(eight_point(re, im)):
                if c > 0:
                    cosine = twiddle[half, c, 0:1, :]
                    sine = twiddle[half, c, 1:2, :]
                    a, b = a * cosine + b * sine, b * cosine - a * sine
                for comp, value in enumerate((a, b)):
                    lanes = slice((2 * half + comp) * LANES, (2 * half + comp + 1) * LANES)
                    top = value.astype(jnp.bfloat16)
                    high[c, rows, lanes] = top
                    low[c, rows, lanes] = (value - top.astype(jnp.float32)).astype(jnp.bfloat16)
            return carry

        lax.fori_loop(0, 144 // TILE, fold, 0)

    copies[2].wait()
    for c in range(NJ):
        a = high[c]
        value = (
            jnp.dot(a, main[0], preferred_element_type=jnp.float32)
            + jnp.dot(low[c], main[0], preferred_element_type=jnp.float32)
            + jnp.dot(a, main[1], preferred_element_type=jnp.float32)
        )
        for part in range(4):
            piece = value[:, part * LANES : (part + 1) * LANES]
            if c % 4 > 0:
                piece = pltpu.roll(piece, 32 * (c % 4), 1)
            for group in range(18):
                mixed[c, part, pl.ds(group, 8, stride=18), :] = piece[8 * group : 8 * group + 8]

    copies[3].wait()
    slot = lax.broadcasted_iota(jnp.int32, (144, LANES), 1) // 32
    stores = []
    for t in range(4):
        for comp in range(2):
            for upper in range(2):
                part = 2 * comp + upper
                for group in range(2):
                    value = mixed[4 * group, part]
                    for c in range(1, 4):
                        value = jnp.where(slot == (c + t) % 4, mixed[4 * group + c, part], value)
                    top = value.astype(jnp.bfloat16)
                    start = part * 144
                    columns = slice(group * LANES, (group + 1) * LANES)
                    woven[start : start + 144, columns] = top
                    woven[start + 576 : start + 720, columns] = (value - top.astype(jnp.float32)).astype(jnp.bfloat16)
        product = jnp.dot(woven[...], weave[t], preferred_element_type=jnp.float32)
        product = product[:576] + product[576:]
        for comp in range(2):
            for upper in range(2):
                tile = 4 * upper + t
                width = min(256, NY - 256 * tile)
                start = (2 * comp + upper) * 144
                lanes = slice(256 * tile, 256 * tile + width)
                out[comp, :, lanes] = product[start : start + 144, :width]
                stores.append(pltpu.make_async_copy(out.at[comp, :, lanes], result.at[comp, field, :, lanes], out_sem))
                stores[-1].start()
    for store in stores:
        store.wait()


def y_transform(field, arrays, before):
    twiddle, main, weave = y_tables()
    anywhere = pl.BlockSpec(memory_space=pltpu.HBM)
    local = pl.BlockSpec(memory_space=pltpu.VMEM)
    inputs = [*arrays, jnp.asarray(twiddle), jnp.asarray(main), jnp.asarray(weave)]
    in_specs = [anywhere] * len(arrays) + [local] + [anywhere] * 2
    aliases = {}
    if before is not None:
        aliases = {len(inputs): 0}
        inputs.append(before)
        in_specs.append(anywhere)
    return pl.pallas_call(
        functools.partial(y_kernel, len(arrays), field),
        in_specs=in_specs,
        out_specs=anywhere,
        out_shape=jax.ShapeDtypeStruct((2, 2, 144, NY), jnp.float32),
        scratch_shapes=[
            pltpu.VMEM((2, NJ, 2, 144, LANES), jnp.float32),
            pltpu.VMEM((NJ, 144, 512), jnp.bfloat16),
            pltpu.VMEM((NJ, 144, 512), jnp.bfloat16),
            pltpu.VMEM((NJ, 4, 144, LANES), jnp.float32),
            pltpu.VMEM((1152, 256), jnp.bfloat16),
            pltpu.VMEM((2, 512, 512), jnp.bfloat16),
            pltpu.VMEM((4, 256, 256), jnp.bfloat16),
            pltpu.VMEM((2, 144, NY), jnp.float32),
            pltpu.SemaphoreType.DMA((4,)),
            pltpu.SemaphoreType.DMA,
        ],
        input_output_aliases=aliases,
        compiler_params=compiler_params(),
        cost_estimate=LIGHT,
        name="y_transform",
    )(*inputs)


def shift(dh, dz, dc):
    pairs = []
    for hi in range(2):
        for z in range(NZ):
            for core in range(2):
                to = (hi + dh) % 2 * 16 + (z + dz) % NZ * 2 + (core + dc) % 2
                pairs.append((hi * 16 + z * 2 + core, to))
    return pairs


def over_y(blocks):
    blocks = blocks.reshape(NJ, -1, 2, 144, LANES)
    return lax.all_to_all(blocks, "gy", split_axis=0, concat_axis=0, tiled=True)


def over_xh(parts):
    return parts[:1] + [lax.ppermute(part, "gx", shift(dh, 0, dc)) for (dh, dc), part in zip(PARTNERS[1:], parts[1:])]


def over_z(sends, order):
    return {dz: lax.ppermute(sends[dz - 1], "gx", shift(0, dz, 0)) for dz in order}


def listed(received):
    return [received[dz] for dz in range(1, NZ)]


def body(fields):
    me = lax.axis_index("gx")
    place = jnp.stack([me // 16, me // 2 % NZ, me % 2]).astype(jnp.int32)
    fields = fields.reshape(2, NZ, 2, 2, STRIP, ROWS)
    first = pack(jnp.zeros(3, jnp.int32), fields, 0, [])[0]
    rest = list(pack(place, fields, 1, [first]))
    first = first.reshape(32, 2, STRIP, LANES)
    first = lax.all_to_all(first, "gx", split_axis=0, concat_axis=0, tiled=True)
    parts = [over_xh(rest[:4]), over_xh(rest[4:])]
    sends = [list(pack_z(place, part, [])) for part in parts]
    second = over_z(sends[0], (1, 7, 2, 6))
    first, sends, second = lax.optimization_barrier((first, sends, second))
    flying = over_z(sends[0], (4,))
    x01 = x_transform(place, [first], [], 2 * 10**10)
    x01, sends, flying = lax.optimization_barrier((x01, sends, flying))
    g01 = over_y(x01)
    second |= flying | over_z(sends[0], (3, 5))
    flying = over_z(sends[1], (4, 2, 6))
    third = over_z(sends[1], (3, 5, 1, 7))
    x2 = x_transform(place, parts[0] + listed(second), [], 2 * 10**10)
    x2, flying = lax.optimization_barrier((x2, flying))
    third |= flying
    g01, x2 = lax.optimization_barrier((g01, x2))
    g2 = over_y(x2)
    x3 = x_transform(place, parts[1] + listed(third), [x2], 2 * 10**11)
    g2, x3 = lax.optimization_barrier((g2, x3))
    g3 = over_y(x3)
    result = y_transform(0, [g01], None)
    return y_transform(1, [g2, g3], result)


def solution(mesh):
    in_specs = (P(None, "gx", "gy"),)
    out_specs = P(None, "gx", "gy", None)
    return jax.shard_map(body, mesh=mesh, in_specs=in_specs, out_specs=out_specs, check_vma=False)
```
